32 devices in a mesh: section: 2 (over y), expert: 16 (over z, x, core).
Axes of the slice: x: 2, y: 2, z: 4, core: 2. Of those that a mesh axis runs over, the one named last changes fastest.
Arguments:
- in_flight: bfloat16 [2, 1024, 2048], P('section', 'expert'), may hold values from -6 to 6
- entering: bfloat16 [1, 1024, 2048], P(None, 'expert'), may hold values from -6 to 6
- norm_gain: bfloat16 [2, 2048], P('section'), may hold values from 0.5 to 1.5
- w_gate: bfloat16 [2, 16, 2048, 768], P('section', 'expert'), may hold values from -0.125 to 0.125
- w_up: bfloat16 [2, 16, 2048, 768], P('section', 'expert'), may hold values from -0.125 to 0.125
- w_down: bfloat16 [2, 16, 768, 2048], P('section', 'expert'), may hold values from -0.21875 to 0.21875
- routes: int32 [2, 2, 1024, 8], P('section', None, 'expert'), may hold values from 0 to 15, all different within a row; in each aligned block of 32 rows (0 to 31, 32 to 63, ..., all dimensions but the last counted through in order) at most 24 rows name the same one
- combine_weight: float32 [2, 2, 1024, 8], P('section', None, 'expert'), may hold values from 0.2 to 0.6
Outputs:
- trace: bfloat16 [2, 2, 1024, 2048], P(None, 'section', 'expert')
The draws below stay inside these ranges and needn't reach their ends.
Inputs may be any that keep to these rules, and one draw needn't show every extreme that they name: `routes`: each row names 8 different experts. In each aligned block of 32 rows (all leading dimensions taken together, in order) no expert is named by more than 24 rows, a bound that some block reaches.
All inputs are finite; a program needn't handle non-finite values.
Results may differ from the reference program's by a relative error of at most 0.0085.
Values may be sent and summed in bfloat16 or wider, within the bound.
A program may use at most 128 MiB of HBM per device.

```python
import math
import jax
import jax.numpy as jnp
import numpy as np
from jax import lax

D = 2048
FF = 768
TOPK = 8
TICKS = 2
LAYERS = 2
EXPERTS = 16
TOKENS = 1024
TOK_HALF = 32
CAP = 24
N_EXPERT = 16


def block_levels(stream_key, shape, cuts, smallest, high):
    def one(axis_at, shards_of):
        heights = jax.random.uniform(jax.random.fold_in(jax.random.fold_in(stream_key, 6), axis_at), (shards_of,), jnp.float32, smallest / len(cuts), high / len(cuts))
        return jnp.repeat(jnp.exp(heights), shape[axis_at] // shards_of).reshape((-1,) + (1,) * (len(shape) - axis_at - 1))

    loudness = one(*cuts[0])
    for cut in cuts[1:]:
        loudness = loudness * one(*cut)
    return loudness


def shared_out(stream_key, own, number, rows, number_of, top, bound, skew):
    ranking = jax.random.permutation(stream_key, number_of)
    crowded, usual = load_shares(number_of, rows * top, bound, skew, True), load_shares(number_of, rows * top, bound, skew, False)
    places = jnp.arange(number_of)

    def named(tallies, turn):
        used = int((tallies > 0).sum())
        fixed = max(1, used // 4)
        shifted = fixed + (places - fixed + turn * (used - fixed)) % max(1, number_of - fixed)
        return jnp.zeros((number_of,), jnp.int32).at[ranking[jnp.where(places < fixed, places, shifted)]].set(jnp.asarray(tallies, jnp.int32))

    tallies = jnp.where(number % 4 == 0, named(crowded, number // 4), named(usual, number - number // 4 - 1))
    mixed = jax.random.permutation(jax.random.fold_in(own, 3), number_of)
    source_of, receiver = mixed[0:number_of // 2 * 2:2], mixed[1:number_of // 2 * 2:2]
    room = jnp.minimum(tallies[source_of] - 1, bound - tallies[receiver]) // 2
    room = jnp.where((source_of == ranking[0]) | (receiver == ranking[0]) | (tallies[receiver] == 0), 0, jnp.maximum(room, 0))
    shifted = jax.random.randint(jax.random.fold_in(own, 4), (number_of // 2,), 0, 1 << 20) % (room + 1)
    tallies = tallies.at[source_of].add(-shifted).at[receiver].add(shifted)
    members = jnp.searchsorted(jnp.cumsum(tallies), jnp.arange(rows * top), side="right").astype(jnp.int32)
    table = members.reshape(top, rows).T
    table = table[jax.random.permutation(jax.random.fold_in(own, 1), rows)]
    turn = jax.random.randint(jax.random.fold_in(own, 2), (rows, 1), 0, top)
    return jnp.take_along_axis(table, (jnp.arange(top)[None, :] + turn) % top, axis=1)


def load_shares(count, total, bound, slope, full):
    loads = [(1 << 20) // math.isqrt(rank ** slope) + 1 for rank in range(1, count + 1)]
    largest = bound if full else min(bound, max(-(-total // count), total * loads[0] // sum(loads)))
    least = 1 if total - largest >= count - 1 else 0
    counts, surplus = [largest] + [least] * (count - 1), total - largest - least * (count - 1)
    while surplus > 0:
        candidates = [i for i in range(1, count) if counts[i] < largest] or [i for i in range(1, count) if counts[i] < bound]
        mass, budget = sum([loads[i] for i in candidates]), surplus
        for i in candidates:
            extra = min(bound - counts[i], max(1, budget * loads[i] // mass), surplus)
            counts[i] = counts[i] + extra
            surplus = surplus - extra
    return np.array(counts)


def gaussian(key, dims, scale, most, cuts=(), held_as=jnp.bfloat16):
    values = jax.random.normal(key, dims, jnp.float32) * scale
    if len(cuts) > 0:
        values = block_levels(key, dims, cuts, -0.22, 0.18) * values
    return jnp.clip(values, min=-most, max=most).astype(held_as)


def setup_inputs(seed: int = 0) -> dict:
    streams_of = jax.random.split(jax.random.key(seed), 9)
    in_flight = gaussian(streams_of[0], (LAYERS, TOKENS, D), 1.0, 6.0, ((0, 2), (1, 16)))
    entering = gaussian(streams_of[1], (TICKS - 1, TOKENS, D), 1.0, 6.0, ((1, 16),))
    norm_gain = jnp.clip(1.0 + 0.1 * jax.random.normal(streams_of[2], (LAYERS, D), jnp.float32), 0.5, 1.5).astype(jnp.bfloat16)
    w_gate = gaussian(streams_of[3], (LAYERS, EXPERTS, D, FF), D ** -0.5, 0.125, ((0, 2), (1, 16)))
    w_up = gaussian(streams_of[4], (LAYERS, EXPERTS, D, FF), D ** -0.5, 0.125, ((0, 2), (1, 16)))
    w_down = gaussian(streams_of[5], (LAYERS, EXPERTS, FF, D), FF ** -0.5, 0.21875, ((0, 2), (1, 16)))
    routes_keys = jax.random.split(jax.random.fold_in(streams_of[6], 1), LAYERS * TICKS * TOKENS // TOK_HALF)
    routes_turns = jax.random.permutation(jax.random.fold_in(streams_of[6], 3), LAYERS * TICKS * TOKENS // TOK_HALF)
    routes = jax.vmap(lambda own, number: shared_out(jax.random.fold_in(streams_of[6], 2), own, number, TOK_HALF, EXPERTS, TOPK, CAP, 1))(routes_keys, routes_turns).reshape((LAYERS, TICKS, TOKENS, TOPK))
    combine_weight = jnp.clip(0.2 + 0.400000021 * jax.random.uniform(streams_of[7], (LAYERS, TICKS, TOKENS, TOPK), jnp.float32) ** block_levels(streams_of[7], (LAYERS, TICKS, TOKENS, TOPK), ((0, 2), (2, 16)), -0.2, 0.2), 0.2, 0.6)
    return dict(in_flight=in_flight, entering=entering, norm_gain=norm_gain, w_gate=w_gate, w_up=w_up, w_down=w_down, routes=routes, combine_weight=combine_weight)


EPSILON = 1e-06

def norm_rows(hidden_rows, norm_gain):
    as_float = hidden_rows.astype(jnp.float32)
    inv_scale = lax.rsqrt(lax.optimization_barrier(jnp.mean(as_float * as_float, axis=-1, keepdims=True)) + EPSILON)
    return (as_float * inv_scale * norm_gain.astype(jnp.float32)).astype(jnp.bfloat16)

def apply_layer(hidden_rows, norm_gain, route_ids, combine, gate_w, up_w, down_w):
    normed = norm_rows(hidden_rows, norm_gain)
    row_total = hidden_rows.shape[0]
    top_count = route_ids.shape[-1]
    flat_routes = route_ids.reshape(-1).astype(jnp.int32)
    flat_weights = combine.reshape(-1)
    most_rows = min(row_total * top_count, 2 * CAP * N_EXPERT)

    def per_expert(running, pieces):
        expert_id, gate_one, up_one, down_one = pieces
        hit_mask = flat_routes == expert_id
        order = jnp.argsort(jnp.where(hit_mask, 0, 1).astype(jnp.int32), stable=True)[:most_rows].astype(jnp.int32)
        chosen = hit_mask[order]
        token_ids = (order // top_count).astype(jnp.int32)
        inputs = normed[token_ids]
        gate_sum = jnp.dot(inputs, gate_one, preferred_element_type=jnp.float32)
        up_sum = jnp.dot(inputs, up_one, preferred_element_type=jnp.float32)
        hidden = (jax.nn.silu(gate_sum) * up_sum).astype(jnp.bfloat16)
        output = jnp.dot(hidden, down_one, preferred_element_type=jnp.float32).astype(jnp.bfloat16)
        scales = jnp.where(chosen, flat_weights[order], jnp.zeros((), flat_weights.dtype))
        scaled = scales[:, None].astype(jnp.float32) * output.astype(jnp.float32)
        return (running.at[token_ids].add(scaled), None)
    start = jnp.zeros((row_total, hidden_rows.shape[1]), jnp.float32)
    expert_ids = jnp.arange(EXPERTS, dtype=jnp.int32)
    summed = lax.scan(per_expert, start, (expert_ids, gate_w, up_w, down_w))[0]
    return (hidden_rows.astype(jnp.float32) + summed).astype(jnp.bfloat16)

def reference(in_flight, entering, norm_gain, w_gate, w_up, w_down, routes, combine_weight):
    carried = [in_flight[section_id] for section_id in range(LAYERS)]
    traced = []
    for tick_index in range(TICKS):
        outputs_now = [apply_layer(carried[section_id], norm_gain[section_id], routes[section_id, tick_index], combine_weight[section_id, tick_index], w_gate[section_id], w_up[section_id], w_down[section_id]) for section_id in range(LAYERS)]
        traced.append(jnp.stack(outputs_now))
        if tick_index + 1 < TICKS:
            carried = [entering[tick_index]] + outputs_now[:-1]
    return jnp.stack(traced)
```

```python
import jax
import jax.numpy as jnp
from jax import lax
from jax.sharding import PartitionSpec as P

TICKS = 2
EPSILON = 1e-06


def passed_along(x, axis, by):
    devices = lax.axis_size(axis)
    pairs = [(i, i + by) for i in range(devices) if 0 <= i + by < devices]
    return lax.ppermute(x, axis, pairs)


def rms_normed(hidden_rows, norm_gain):
    as_float = hidden_rows.astype(jnp.float32)
    inv_scale = lax.rsqrt(jnp.mean(as_float * as_float, axis=-1, keepdims=True) + EPSILON)
    return (as_float * inv_scale * norm_gain.astype(jnp.float32)).astype(jnp.bfloat16)


def expert_weights(routes, combine, experts):
    hits = routes[..., None] == jnp.arange(experts, dtype=jnp.int32)
    return jnp.sum(jnp.where(hits, combine[..., None], 0.0), axis=-2)


def gathered_layer(hidden_rows, norm_gain, scales, gate_w, up_w, down_w):
    normed = rms_normed(hidden_rows, norm_gain)
    inputs = lax.all_gather(normed, "expert", axis=0, tiled=True)
    gate_sum = jnp.dot(inputs, gate_w, preferred_element_type=jnp.float32)
    up_sum = jnp.dot(inputs, up_w, preferred_element_type=jnp.float32)
    hidden = (jax.nn.silu(gate_sum) * up_sum).astype(jnp.bfloat16)
    result = jnp.dot(hidden, down_w, preferred_element_type=jnp.float32)
    scaled = (result * scales).astype(jnp.bfloat16)
    summed = lax.psum_scatter(scaled, "expert", scatter_dimension=0, tiled=True)
    return (hidden_rows.astype(jnp.float32) + summed.astype(jnp.float32)).astype(jnp.bfloat16)


def local(in_flight, entering, norm_gain, w_gate, w_up, w_down, routes, combine_weight):
    section_index = lax.axis_index("section")
    experts = lax.axis_size("expert") * w_gate.shape[1]
    spread = expert_weights(routes[0], combine_weight[0], experts)
    mine = lax.all_to_all(spread, "expert", split_axis=2, concat_axis=1, tiled=True)
    carried = in_flight[0]
    traced = []
    for tick_index in range(TICKS):
        layer_out = gathered_layer(
            carried, norm_gain[0], mine[tick_index], w_gate[0, 0], w_up[0, 0], w_down[0, 0]
        )
        traced.append(layer_out)
        if tick_index + 1 < TICKS:
            shifted = passed_along(layer_out, "section", 1)
            carried = jnp.where(section_index == 0, entering[tick_index], shifted)
    return jnp.stack(traced)[:, None]


def solution(mesh):
    placed = (
        P("section", "expert", None),
        P(None, "expert", None),
        P("section", None),
        P("section", "expert", None, None),
        P("section", "expert", None, None),
        P("section", "expert", None, None),
        P("section", None, "expert", None),
        P("section", None, "expert", None),
    )
    return jax.shard_map(
        local,
        mesh=mesh,
        in_specs=placed,
        out_specs=P(None, "section", "expert", None),
        check_vma=False,
    )
```

```python
import jax
import jax.numpy as jnp
from jax import lax
from jax.experimental import pallas as pl
from jax.experimental.pallas import tpu as pltpu
from jax.sharding import PartitionSpec as P

TICKS = 2
EPSILON = 1e-06


def passed_along(x, axis, by):
    devices = lax.axis_size(axis)
    pairs = [(i, i + by) for i in range(devices) if 0 <= i + by < devices]
    return lax.ppermute(x, axis, pairs)


def rms_normed(hidden_rows, norm_gain):
    as_float = hidden_rows.astype(jnp.float32)
    inv_scale = lax.rsqrt(jnp.mean(as_float * as_float, axis=-1, keepdims=True) + EPSILON)
    return (as_float * inv_scale * norm_gain.astype(jnp.float32)).astype(jnp.bfloat16)


def expert_weights(routes, combine, experts):
    hits = routes[..., None] == jnp.arange(experts, dtype=jnp.int32)
    return jnp.sum(jnp.where(hits, combine[..., None], 0.0), axis=-2)


def gathered_layer(hidden_rows, norm_gain, scales, gate_w, up_w, down_w):
    normed = rms_normed(hidden_rows, norm_gain)
    inputs = lax.all_gather(normed, "expert", axis=0, tiled=True)
    gate_sum = jnp.dot(inputs, gate_w, preferred_element_type=jnp.float32)
    up_sum = jnp.dot(inputs, up_w, preferred_element_type=jnp.float32)
    hidden = (jax.nn.silu(gate_sum) * up_sum).astype(jnp.bfloat16)
    result = jnp.dot(hidden, down_w, preferred_element_type=jnp.float32)
    scaled = (result * scales).astype(jnp.bfloat16)
    summed = lax.psum_scatter(scaled, "expert", scatter_dimension=0, tiled=True)
    return (hidden_rows.astype(jnp.float32) + summed.astype(jnp.float32)).astype(jnp.bfloat16)


NZ = 4


def layers_kernel(
    x_ref, entering_ref, gain_ref, scale_ref, gate_hbm, up_hbm, down_hbm, out_ref,
    gathered, held_next, hidden, part, core_in, chip_sum, x_in, pair_sum, z_in,
    gate_w, up_w, down_w,
    w_sem, zs, zr, xs, xr, cs, cr, ps, pr, qs, qr, ts, tr, hs, hr,
):
    section = lax.axis_index("section")
    me = lax.axis_index("expert")
    core = me % 2
    across = (me // 2) % 2
    z = me // 4
    zpeer = [z, z + 1 - 2 * (z % 2), (z + 2) % 4, 3 - z]

    def expert_id(zz, xx, cc):
        return {"expert": zz * 4 + xx * 2 + cc}

    z_ids = [expert_id(zpeer[d], across, core) for d in range(NZ)]
    x_id = expert_id(z, 1 - across, core)
    c_id = expert_id(z, across, 1 - core)
    s_id = {"section": 1 - section}

    loads = [
        pltpu.make_async_copy(src, dst, w_sem.at[i])
        for i, (src, dst) in enumerate(((gate_hbm, gate_w), (up_hbm, up_w), (down_hbm, down_w)))
    ]
    for load in loads:
        load.start()

    barrier = pltpu.get_barrier_semaphore()
    for peer in z_ids[1:] + [x_id, c_id, s_id]:
        pl.semaphore_signal(barrier, inc=1, device_id=peer, device_id_type=pl.DeviceIdType.MESH)

    sends = []

    def send(src, dst, s_sem, r_sem, peer):
        copy = pltpu.make_async_remote_copy(
            src_ref=src, dst_ref=dst, send_sem=s_sem, recv_sem=r_sem,
            device_id=peer, device_id_type=pl.DeviceIdType.MESH,
        )
        copy.start()
        sends.append(copy)

    def arrived(ref, s_sem, r_sem, peer):
        pltpu.make_async_remote_copy(
            src_ref=ref, dst_ref=ref, send_sem=s_sem, recv_sem=r_sem,
            device_id=peer, device_id_type=pl.DeviceIdType.MESH,
        ).wait_recv()

    def run_tick(t, first):
        rows = x_ref[...] if t == 0 else held_next[...]
        as_float = rows.astype(jnp.float32)
        inv = lax.rsqrt(jnp.mean(as_float * as_float, axis=-1, keepdims=True) + EPSILON)
        own = gathered.at[t, z, across, core]
        own[...] = (as_float * inv * gain_ref[...].astype(jnp.float32)).astype(jnp.bfloat16)
        if first:
            pl.semaphore_wait(barrier, NZ + 2)
        for d in range(1, NZ):
            send(own, own, zs.at[t, d], zr.at[t, d], z_ids[d])

        def stage_a(k):
            mine = gathered.at[t, zpeer[k], across, core]
            if k:
                arrived(mine, zs.at[t, k], zr.at[t, k], z_ids[k])
            send(mine, mine, xs.at[t, k], xr.at[t, k], x_id)
            send(mine, mine, cs.at[t, 0, k], cr.at[t, 0, k], c_id)

        def stage_b(k):
            other = gathered.at[t, zpeer[k], 1 - across, core]
            arrived(other, xs.at[t, k], xr.at[t, k], x_id)
            send(other, other, cs.at[t, 1, k], cr.at[t, 1, k], c_id)

        def stage_c(k):
            arrived(gathered.at[t, zpeer[k], across, 1 - core], cs.at[t, 0, k], cr.at[t, 0, k], c_id)
            arrived(
                gathered.at[t, zpeer[k], 1 - across, 1 - core], cs.at[t, 1, k], cr.at[t, 1, k], c_id
            )
            if first and k == 0:
                for load in loads:
                    load.wait()
            group = gathered.at[t, zpeer[k]]
            count = 4 * group.shape[2]
            height = group.shape[2]

            def up_tile(i, carry):
                columns = pl.ds(pl.multiple_of(i * 256, 256), 256)
                inputs = group[...].reshape(count, group.shape[3])
                g = jnp.dot(inputs, gate_w[:, columns], preferred_element_type=jnp.float32)
                u = jnp.dot(inputs, up_w[:, columns], preferred_element_type=jnp.float32)
                hidden[:, columns] = (g / (1.0 + jnp.exp(-g)) * u).astype(jnp.bfloat16)
                return carry

            lax.fori_loop(0, hidden.shape[1] // 256, up_tile, 0)
            start = pl.multiple_of(zpeer[k] * count, count)
            scale = scale_ref[t, pl.ds(start, count), :]

            def down_tile(i, carry):
                columns = pl.ds(pl.multiple_of(i * 256, 256), 256)
                r = jnp.dot(hidden[...], down_w[:, columns], preferred_element_type=jnp.float32)
                r = (r * scale).astype(jnp.bfloat16)
                for xx in range(2):
                    for cc in range(2):
                        at = (xx * 2 + cc) * height
                        part[t, k, cc, xx, :, columns] = r[at : at + height]
                return carry

            lax.fori_loop(0, down_w.shape[1] // 256, down_tile, 0)
            send(part.at[t, k, 1 - core], core_in.at[t, k], ps.at[t, k], pr.at[t, k], c_id)

        def stage_d(k):
            arrived(core_in.at[t, k], ps.at[t, k], pr.at[t, k], c_id)
            chip_sum[t, k] = (
                part[t, k, core].astype(jnp.float32) + core_in[t, k].astype(jnp.float32)
            ).astype(jnp.bfloat16)
            send(chip_sum.at[t, k, 1 - across], x_in.at[t, k], qs.at[t, k], qr.at[t, k], x_id)

        def stage_e(k):
            arrived(x_in.at[t, k], qs.at[t, k], qr.at[t, k], x_id)
            pair_sum[t, k] = (
                chip_sum[t, k, across].astype(jnp.float32) + x_in[t, k].astype(jnp.float32)
            ).astype(jnp.bfloat16)
            if k:
                send(pair_sum.at[t, k], z_in.at[t, k], ts.at[t, k], tr.at[t, k], z_ids[k])

        for step in range(NZ + 4):
            for lag, stage in ((0, stage_a), (1, stage_b), (3, stage_d), (4, stage_e), (2, stage_c)):
                if 0 <= step - lag < NZ:
                    stage(step - lag)

        total = as_float + pair_sum[t, 0].astype(jnp.float32)
        for k in range(1, NZ):
            arrived(z_in.at[t, k], ts.at[t, k], tr.at[t, k], z_ids[k])
            total = total + z_in[t, k].astype(jnp.float32)
        out_ref[t] = total.astype(jnp.bfloat16)

    run_tick(0, True)
    carry = pltpu.make_async_remote_copy(
        src_ref=out_ref.at[0], dst_ref=held_next, send_sem=hs, recv_sem=hr,
        device_id=s_id, device_id_type=pl.DeviceIdType.MESH,
    )

    @pl.when(section == 0)
    def _():
        carry.start()
        held_next[...] = entering_ref[...]

    @pl.when(section == 1)
    def _():
        carry.wait_recv()

    run_tick(1, False)

    @pl.when(section == 0)
    def _():
        carry.wait_send()

    for copy in sends:
        copy.wait_send()


def layers_call(held, entering, gain, scales, gate_w, up_w, down_w):
    rows, width = held.shape
    inner = gate_w.shape[1]
    bf16 = jnp.bfloat16
    dma = pltpu.SemaphoreType.DMA
    vmem = pl.BlockSpec(memory_space=pltpu.VMEM)
    hbm = pl.BlockSpec(memory_space=pl.ANY)
    tall = TICKS * 16 * rows
    return pl.pallas_call(
        layers_kernel,
        out_shape=jax.ShapeDtypeStruct((TICKS, rows, width), bf16),
        in_specs=[vmem] * 4 + [hbm] * 3,
        out_specs=vmem,
        scratch_shapes=[
            pltpu.VMEM((TICKS, NZ, 2, 2, rows, width), bf16),
            pltpu.VMEM((rows, width), bf16),
            pltpu.VMEM((4 * rows, inner), bf16),
            pltpu.VMEM((TICKS, NZ, 2, 2, rows, width), bf16),
            pltpu.VMEM((TICKS, NZ, 2, rows, width), bf16),
            pltpu.VMEM((TICKS, NZ, 2, rows, width), bf16),
            pltpu.VMEM((TICKS, NZ, rows, width), bf16),
            pltpu.VMEM((TICKS, NZ, rows, width), bf16),
            pltpu.VMEM((TICKS, NZ, rows, width), bf16),
            pltpu.VMEM(gate_w.shape, bf16),
            pltpu.VMEM(up_w.shape, bf16),
            pltpu.VMEM(down_w.shape, bf16),
            dma((3,)),
            dma((TICKS, NZ)), dma((TICKS, NZ)),
            dma((TICKS, NZ)), dma((TICKS, NZ)),
            dma((TICKS, 2, NZ)), dma((TICKS, 2, NZ)),
            dma((TICKS, NZ)), dma((TICKS, NZ)),
            dma((TICKS, NZ)), dma((TICKS, NZ)),
            dma((TICKS, NZ)), dma((TICKS, NZ)),
            dma, dma,
        ],
        compiler_params=pltpu.CompilerParams(
            collective_id=0, has_side_effects=True, vmem_limit_bytes=58 * 2**20
        ),
        cost_estimate=pl.CostEstimate(
            flops=6 * tall * width * inner,
            bytes_accessed=6 * width * inner + 8 * rows * width,
            transcendentals=tall * inner,
        ),
    )(held, entering, gain, scales, gate_w, up_w, down_w)


def local(in_flight, entering, norm_gain, w_gate, w_up, w_down, routes, combine_weight):
    section_index = lax.axis_index("section")
    experts = lax.axis_size("expert") * w_gate.shape[1]
    spread = expert_weights(routes[0], combine_weight[0], experts)
    mine = lax.all_to_all(spread, "expert", split_axis=2, concat_axis=1, tiled=True)
    if experts == 4 * NZ and lax.axis_size("section") == 2:
        return layers_call(
            in_flight[0], entering[0], norm_gain, mine, w_gate[0, 0], w_up[0, 0], w_down[0, 0]
        )[:, None]
    carried = in_flight[0]
    traced = []
    for tick_index in range(TICKS):
        layer_out = gathered_layer(
            carried, norm_gain[0], mine[tick_index], w_gate[0, 0], w_up[0, 0], w_down[0, 0]
        )
        traced.append(layer_out)
        if tick_index + 1 < TICKS:
            shifted = passed_along(layer_out, "section", 1)
            carried = jnp.where(section_index == 0, entering[tick_index], shifted)
    return jnp.stack(traced)[:, None]


def solution(mesh):
    placed = (
        P("section", "expert", None),
        P(None, "expert", None),
        P("section", None),
        P("section", "expert", None, None),
        P("section", "expert", None, None),
        P("section", "expert", None, None),
        P("section", None, "expert", None),
        P("section", None, "expert", None),
    )
    return jax.shard_map(
        local,
        mesh=mesh,
        in_specs=placed,
        out_specs=P(None, "section", "expert", None),
        check_vma=False,
    )
```

```python
import jax
import jax.numpy as jnp
from jax import lax
from jax.experimental import pallas as pl
from jax.experimental.pallas import tpu as pltpu
from jax.sharding import PartitionSpec as P

TICKS = 2
EPSILON = 1e-06


def passed_along(x, axis, by):
    devices = lax.axis_size(axis)
    pairs = [(i, i + by) for i in range(devices) if 0 <= i + by < devices]
    return lax.ppermute(x, axis, pairs)


def rms_normed(hidden_rows, norm_gain):
    as_float = hidden_rows.astype(jnp.float32)
    inv_scale = lax.rsqrt(jnp.mean(as_float * as_float, axis=-1, keepdims=True) + EPSILON)
    return (as_float * inv_scale * norm_gain.astype(jnp.float32)).astype(jnp.bfloat16)


def expert_weights(routes, combine, experts):
    hits = routes[..., None] == jnp.arange(experts, dtype=jnp.int32)
    return jnp.sum(jnp.where(hits, combine[..., None], 0.0), axis=-2)


def gathered_layer(hidden_rows, norm_gain, scales, gate_w, up_w, down_w):
    normed = rms_normed(hidden_rows, norm_gain)
    inputs = lax.all_gather(normed, "expert", axis=0, tiled=True)
    gate_sum = jnp.dot(inputs, gate_w, preferred_element_type=jnp.float32)
    up_sum = jnp.dot(inputs, up_w, preferred_element_type=jnp.float32)
    hidden = (jax.nn.silu(gate_sum) * up_sum).astype(jnp.bfloat16)
    result = jnp.dot(hidden, down_w, preferred_element_type=jnp.float32)
    scaled = (result * scales).astype(jnp.bfloat16)
    summed = lax.psum_scatter(scaled, "expert", scatter_dimension=0, tiled=True)
    return (hidden_rows.astype(jnp.float32) + summed.astype(jnp.float32)).astype(jnp.bfloat16)


NZ = 4


def layers_kernel(
    x_ref, entering_ref, gain_ref, spread_ref, gate_hbm, up_hbm, down_hbm, out_ref,
    gathered, held_next, hidden, part, core_in, chip_sum, x_in, pair_sum, z_in,
    gate_w, up_w, down_w, spread_in, scale_ref,
    w_sem, ss, sr, zs, zr, xs, xr, cs, cr, ps, pr, qs, qr, ts, tr, hs, hr,
):
    section = lax.axis_index("section")
    me = lax.axis_index("expert")
    core = me % 2
    across = (me // 2) % 2
    z = me // 4
    inner = ((z + 1) // 2) % 2
    near, skip, mirror = z + 1 - 2 * (z % 2), (z + 2) % 4, 3 - z
    zpeer = [
        z,
        near,
        (1 - inner) * skip + inner * mirror,
        (1 - inner) * mirror + inner * skip,
    ]
    lane = [0, 1, 2 + inner, 3 - inner]
    devices = 4 * NZ

    def expert_id(zz, xx, cc):
        return {"expert": zz * 4 + xx * 2 + cc}

    z_ids = [expert_id(zpeer[d], across, core) for d in range(NZ)]
    x_id = expert_id(z, 1 - across, core)
    c_id = expert_id(z, across, 1 - core)
    s_id = {"section": 1 - section}

    loads = [
        pltpu.make_async_copy(src, dst, w_sem.at[i])
        for i, (src, dst) in enumerate(((gate_hbm, gate_w), (up_hbm, up_w), (down_hbm, down_w)))
    ]
    for load in loads:
        load.start()

    barrier = pltpu.get_barrier_semaphore()
    others = [{"expert": (me + d) % devices} for d in range(1, devices)]
    for peer in others + [s_id]:
        pl.semaphore_signal(barrier, inc=1, device_id=peer, device_id_type=pl.DeviceIdType.MESH)
    spread_in[me] = spread_ref[me]

    sends = []
    inner_sends = []

    def describe(src, dst, s_sem, r_sem, peer):
        return pltpu.make_async_remote_copy(
            src_ref=src, dst_ref=dst, send_sem=s_sem, recv_sem=r_sem,
            device_id=peer, device_id_type=pl.DeviceIdType.MESH,
        )

    def begin(*args):
        copy = describe(*args)
        copy.start()
        return copy

    def send(*args):
        sends.append(begin(*args))

    def send_inner(*args):
        @pl.when(inner == 1)
        def _():
            begin(*args)

        inner_sends.append(args)

    def arrived(ref, s_sem, r_sem, peer):
        pltpu.make_async_remote_copy(
            src_ref=ref, dst_ref=ref, send_sem=s_sem, recv_sem=r_sem,
            device_id=peer, device_id_type=pl.DeviceIdType.MESH,
        ).wait_recv()

    def run_tick(t, first):
        rows = x_ref[...] if t == 0 else held_next[...]
        as_float = rows.astype(jnp.float32)
        inv = lax.rsqrt(jnp.mean(as_float * as_float, axis=-1, keepdims=True) + EPSILON)
        own = gathered.at[t, z, across, core]
        own[...] = (as_float * inv * gain_ref[...].astype(jnp.float32)).astype(jnp.bfloat16)
        if first:
            pl.semaphore_wait(barrier, devices)
        send(own, own, zs.at[t, 0], zr.at[t, 1], z_ids[1])
        send_inner(own, own, zs.at[t, 1], zr.at[t, 2], z_ids[2])

        def stage_a(k):
            mine = gathered.at[t, zpeer[k], across, core]
            if k:
                arrived(mine, zs.at[t, 0], zr.at[t, k], z_ids[k])
                if k == 1:
                    send_inner(mine, mine, zs.at[t, 2], zr.at[t, 3], z_ids[2])
                else:
                    send_inner(mine, mine, zs.at[t, k + 1], zr.at[t, k], z_ids[1])
            send(mine, mine, xs.at[t, k], xr.at[t, k], x_id)
            send(mine, mine, cs.at[t, 0, k], cr.at[t, 0, k], c_id)

            if first and k == 0:
                for d in range(1, devices):
                    peer = (me + d) % devices
                    send(spread_ref.at[peer], spread_in.at[me], ss.at[d], sr.at[d], {"expert": peer})

        def stage_b(k):
            other = gathered.at[t, zpeer[k], 1 - across, core]
            arrived(other, xs.at[t, k], xr.at[t, k], x_id)
            send(other, other, cs.at[t, 1, k], cr.at[t, 1, k], c_id)

        def stage_c(k):
            arrived(gathered.at[t, zpeer[k], across, 1 - core], cs.at[t, 0, k], cr.at[t, 0, k], c_id)
            arrived(
                gathered.at[t, zpeer[k], 1 - across, 1 - core], cs.at[t, 1, k], cr.at[t, 1, k], c_id
            )
            if first and k == 0:
                for d in range(1, devices):
                    source = (me + devices - d) % devices
                    arrived(spread_in.at[source], ss.at[d], sr.at[d], {"expert": source})
                height = own.shape[0]
                turned = jnp.concatenate([spread_in[b] for b in range(devices)], axis=0).T
                for b in range(devices):
                    for at in range(TICKS):
                        scale_ref[at, b * height : (b + 1) * height, :] = turned[
                            at * height : (at + 1) * height, b : b + 1
                        ]
                for load in loads:
                    load.wait()
            group = gathered.at[t, zpeer[k]]
            count = 4 * group.shape[2]
            height = group.shape[2]

            def up_tile(i, carry):
                columns = pl.ds(pl.multiple_of(i * 256, 256), 256)
                inputs = group[...].reshape(count, group.shape[3])
                g = jnp.dot(inputs, gate_w[:, columns], preferred_element_type=jnp.float32)
                u = jnp.dot(inputs, up_w[:, columns], preferred_element_type=jnp.float32)
                hidden[:, columns] = (g / (1.0 + jnp.exp(-g)) * u).astype(jnp.bfloat16)
                return carry

            lax.fori_loop(0, hidden.shape[1] // 256, up_tile, 0)
            start = pl.multiple_of(zpeer[k] * count, count)
            scale = scale_ref[t, pl.ds(start, count), :]

            def down_tile(i, carry):
                columns = pl.ds(pl.multiple_of(i * 256, 256), 256)
                r = jnp.dot(hidden[...], down_w[:, columns], preferred_element_type=jnp.float32)
                r = (r * scale).astype(jnp.bfloat16)
                for xx in range(2):
                    for cc in range(2):
                        at = (xx * 2 + cc) * height
                        part[t, k, cc, xx, :, columns] = r[at : at + height]
                return carry

            lax.fori_loop(0, down_w.shape[1] // 256, down_tile, 0)
            send(part.at[t, k, 1 - core], core_in.at[t, k], ps.at[t, k], pr.at[t, k], c_id)

        def stage_d(k):
            arrived(core_in.at[t, k], ps.at[t, k], pr.at[t, k], c_id)
            chip_sum[t, k] = (
                part[t, k, core].astype(jnp.float32) + core_in[t, k].astype(jnp.float32)
            ).astype(jnp.bfloat16)
            send(chip_sum.at[t, k, 1 - across], x_in.at[t, k], qs.at[t, k], qr.at[t, k], x_id)

        def stage_e(k):
            arrived(x_in.at[t, k], qs.at[t, k], qr.at[t, k], x_id)
            pair_sum[t, k] = (
                chip_sum[t, k, across].astype(jnp.float32) + x_in[t, k].astype(jnp.float32)
            ).astype(jnp.bfloat16)
            if k:
                send(pair_sum.at[t, k], z_in.at[t, lane[k]], ts.at[t, k], tr.at[t, lane[k]], z_ids[k])

        for step in range(NZ + 4):
            for lag, stage in ((0, stage_a), (1, stage_b), (3, stage_d), (4, stage_e), (2, stage_c)):
                if 0 <= step - lag < NZ:
                    stage(step - lag)

        total = as_float + pair_sum[t, 0].astype(jnp.float32)
        for k in range(1, NZ):
            arrived(z_in.at[t, k], ts.at[t, k], tr.at[t, k], z_ids[k])
            total = total + z_in[t, k].astype(jnp.float32)
        out_ref[t] = total.astype(jnp.bfloat16)

    run_tick(0, True)
    carry = pltpu.make_async_remote_copy(
        src_ref=out_ref.at[0], dst_ref=held_next, send_sem=hs, recv_sem=hr,
        device_id=s_id, device_id_type=pl.DeviceIdType.MESH,
    )

    @pl.when(section == 0)
    def _():
        carry.start()
        held_next[...] = entering_ref[...]

    @pl.when(section == 1)
    def _():
        carry.wait_recv()

    run_tick(1, False)

    @pl.when(section == 0)
    def _():
        carry.wait_send()

    for copy in sends:
        copy.wait_send()

    @pl.when(inner == 1)
    def _():
        for args in inner_sends:
            describe(*args).wait_send()


def layers_call(held, entering, gain, spread, gate_w, up_w, down_w):
    rows, width = held.shape
    inner = gate_w.shape[1]
    bf16 = jnp.bfloat16
    dma = pltpu.SemaphoreType.DMA
    vmem = pl.BlockSpec(memory_space=pltpu.VMEM)
    hbm = pl.BlockSpec(memory_space=pl.ANY)
    tall = TICKS * 16 * rows
    return pl.pallas_call(
        layers_kernel,
        out_shape=jax.ShapeDtypeStruct((TICKS, rows, width), bf16),
        in_specs=[vmem] * 4 + [hbm] * 3,
        out_specs=vmem,
        scratch_shapes=[
            pltpu.VMEM((TICKS, NZ, 2, 2, rows, width), bf16),
            pltpu.VMEM((rows, width), bf16),
            pltpu.VMEM((4 * rows, inner), bf16),
            pltpu.VMEM((TICKS, NZ, 2, 2, rows, width), bf16),
            pltpu.VMEM((TICKS, NZ, 2, rows, width), bf16),
            pltpu.VMEM((TICKS, NZ, 2, rows, width), bf16),
            pltpu.VMEM((TICKS, NZ, rows, width), bf16),
            pltpu.VMEM((TICKS, NZ, rows, width), bf16),
            pltpu.VMEM((TICKS, NZ, rows, width), bf16),
            pltpu.VMEM(gate_w.shape, bf16),
            pltpu.VMEM(up_w.shape, bf16),
            pltpu.VMEM(down_w.shape, bf16),
            pltpu.VMEM((4 * NZ, 1, TICKS * rows), jnp.float32),
            pltpu.VMEM((TICKS, 4 * NZ * rows, 1), jnp.float32),
            dma((3,)),
            dma((4 * NZ,)), dma((4 * NZ,)),
            dma((TICKS, NZ + 1)), dma((TICKS, NZ)),
            dma((TICKS, NZ)), dma((TICKS, NZ)),
            dma((TICKS, 2, NZ)), dma((TICKS, 2, NZ)),
            dma((TICKS, NZ)), dma((TICKS, NZ)),
            dma((TICKS, NZ)), dma((TICKS, NZ)),
            dma((TICKS, NZ)), dma((TICKS, NZ)),
            dma, dma,
        ],
        compiler_params=pltpu.CompilerParams(
            collective_id=0, has_side_effects=True, vmem_limit_bytes=58 * 2**20
        ),
        cost_estimate=pl.CostEstimate(
            flops=6 * tall * width * inner,
            bytes_accessed=6 * width * inner + 8 * rows * width,
            transcendentals=tall * inner,
        ),
    )(held, entering, gain, spread, gate_w, up_w, down_w)


def local(in_flight, entering, norm_gain, w_gate, w_up, w_down, routes, combine_weight):
    section_index = lax.axis_index("section")
    experts = lax.axis_size("expert") * w_gate.shape[1]
    spread = expert_weights(routes[0], combine_weight[0], experts)
    if experts == 4 * NZ and lax.axis_size("section") == 2:
        return layers_call(
            in_flight[0], entering[0], norm_gain, spread.reshape(-1, experts).T[:, None],
            w_gate[0, 0], w_up[0, 0], w_down[0, 0],
        )[:, None]
    mine = lax.all_to_all(spread, "expert", split_axis=2, concat_axis=1, tiled=True)
    carried = in_flight[0]
    traced = []
    for tick_index in range(TICKS):
        layer_out = gathered_layer(
            carried, norm_gain[0], mine[tick_index], w_gate[0, 0], w_up[0, 0], w_down[0, 0]
        )
        traced.append(layer_out)
        if tick_index + 1 < TICKS:
            shifted = passed_along(layer_out, "section", 1)
            carried = jnp.where(section_index == 0, entering[tick_index], shifted)
    return jnp.stack(traced)[:, None]


def solution(mesh):
    placed = (
        P("section", "expert", None),
        P(None, "expert", None),
        P("section", None),
        P("section", "expert", None, None),
        P("section", "expert", None, None),
        P("section", "expert", None, None),
        P("section", None, "expert", None),
        P("section", None, "expert", None),
    )
    return jax.shard_map(
        local,
        mesh=mesh,
        in_specs=placed,
        out_specs=P(None, "section", "expert", None),
        check_vma=False,
    )
```

```python
import jax
import jax.numpy as jnp
from jax import lax
from jax.experimental import pallas as pl
from jax.experimental.pallas import tpu as pltpu
from jax.sharding import PartitionSpec as P

TICKS = 2
EPSILON = 1e-06


def passed_along(x, axis, by):
    devices = lax.axis_size(axis)
    pairs = [(i, i + by) for i in range(devices) if 0 <= i + by < devices]
    return lax.ppermute(x, axis, pairs)


def rms_normed(hidden_rows, norm_gain):
    as_float = hidden_rows.astype(jnp.float32)
    inv_scale = lax.rsqrt(jnp.mean(as_float * as_float, axis=-1, keepdims=True) + EPSILON)
    return (as_float * inv_scale * norm_gain.astype(jnp.float32)).astype(jnp.bfloat16)


def expert_weights(routes, combine, experts):
    hits = routes[..., None] == jnp.arange(experts, dtype=jnp.int32)
    return jnp.sum(jnp.where(hits, combine[..., None], 0.0), axis=-2)


def gathered_layer(hidden_rows, norm_gain, scales, gate_w, up_w, down_w):
    normed = rms_normed(hidden_rows, norm_gain)
    inputs = lax.all_gather(normed, "expert", axis=0, tiled=True)
    gate_sum = jnp.dot(inputs, gate_w, preferred_element_type=jnp.float32)
    up_sum = jnp.dot(inputs, up_w, preferred_element_type=jnp.float32)
    hidden = (jax.nn.silu(gate_sum) * up_sum).astype(jnp.bfloat16)
    result = jnp.dot(hidden, down_w, preferred_element_type=jnp.float32)
    scaled = (result * scales).astype(jnp.bfloat16)
    summed = lax.psum_scatter(scaled, "expert", scatter_dimension=0, tiled=True)
    return (hidden_rows.astype(jnp.float32) + summed.astype(jnp.float32)).astype(jnp.bfloat16)


NZ = 4


def layers_kernel(
    x_ref, entering_ref, gain_ref, spread_ref, gate_hbm, up_hbm, down_hbm, out_ref,
    gathered, held_next, hidden, part, core_in, chip_sum, x_in, pair_sum, z_in,
    gate_w, up_w, down_w, spread_in, scale_ref,
    w_sem, ss, sr, zs, zr, xs, xr, cs, cr, ps, pr, qs, qr, ts, tr, hs, hr,
):
    section = lax.axis_index("section")
    me = lax.axis_index("expert")
    core = me % 2
    across = (me // 2) % 2
    z = me // 4
    inner = ((z + 1) // 2) % 2
    near, skip, mirror = z + 1 - 2 * (z % 2), (z + 2) % 4, 3 - z
    zpeer = [
        z,
        near,
        (1 - inner) * skip + inner * mirror,
        (1 - inner) * mirror + inner * skip,
    ]
    lane = [0, 1, 2 + inner, 3 - inner]
    devices = 4 * NZ

    def expert_id(zz, xx, cc):
        return {"expert": zz * 4 + xx * 2 + cc}

    z_ids = [expert_id(zpeer[d], across, core) for d in range(NZ)]
    x_id = expert_id(z, 1 - across, core)
    c_id = expert_id(z, across, 1 - core)
    s_id = {"section": 1 - section}

    loads = [
        pltpu.make_async_copy(src, dst, w_sem.at[i])
        for i, (src, dst) in enumerate(((gate_hbm, gate_w), (up_hbm, up_w), (down_hbm, down_w)))
    ]
    for load in loads:
        load.start()

    barrier = pltpu.get_barrier_semaphore()
    others = [{"expert": (me + d) % devices} for d in range(1, devices)]
    for peer in others + [s_id]:
        pl.semaphore_signal(barrier, inc=1, device_id=peer, device_id_type=pl.DeviceIdType.MESH)
    spread_in[me] = spread_ref[me]

    sends = []
    inner_sends = []

    def describe(src, dst, s_sem, r_sem, peer):
        return pltpu.make_async_remote_copy(
            src_ref=src, dst_ref=dst, send_sem=s_sem, recv_sem=r_sem,
            device_id=peer, device_id_type=pl.DeviceIdType.MESH,
        )

    def begin(*args):
        copy = describe(*args)
        copy.start()
        return copy

    def send(*args):
        sends.append(begin(*args))

    def send_inner(*args):
        @pl.when(inner == 1)
        def _():
            begin(*args)

        inner_sends.append(args)

    def arrived(ref, s_sem, r_sem, peer):
        pltpu.make_async_remote_copy(
            src_ref=ref, dst_ref=ref, send_sem=s_sem, recv_sem=r_sem,
            device_id=peer, device_id_type=pl.DeviceIdType.MESH,
        ).wait_recv()

    def run_tick(t, first):
        rows = x_ref[...] if t == 0 else held_next[...]
        as_float = rows.astype(jnp.float32)
        inv = lax.rsqrt(jnp.mean(as_float * as_float, axis=-1, keepdims=True) + EPSILON)
        own = gathered.at[t, z, across, core]
        own[...] = (as_float * inv * gain_ref[...].astype(jnp.float32)).astype(jnp.bfloat16)
        if first:
            pl.semaphore_wait(barrier, devices)
        send(own, own, zs.at[t, 0], zr.at[t, 1], z_ids[1])
        send_inner(own, own, zs.at[t, 1], zr.at[t, 2], z_ids[2])

        def stage_a(k):
            mine = gathered.at[t, zpeer[k], across, core]
            if k:
                arrived(mine, zs.at[t, 0], zr.at[t, k], z_ids[k])
                if k == 1:
                    send_inner(mine, mine, zs.at[t, 2], zr.at[t, 3], z_ids[2])
                else:
                    send_inner(mine, mine, zs.at[t, k + 1], zr.at[t, k], z_ids[1])
            send(mine, mine, xs.at[t, k], xr.at[t, k], x_id)
            send(mine, mine, cs.at[t, 0, k], cr.at[t, 0, k], c_id)

            if first and k == 0:
                for d in range(1, devices):
                    peer = (me + d) % devices
                    send(spread_ref.at[peer], spread_in.at[me], ss.at[d], sr.at[d], {"expert": peer})

        def stage_b(k):
            other = gathered.at[t, zpeer[k], 1 - across, core]
            arrived(other, xs.at[t, k], xr.at[t, k], x_id)
            send(other, other, cs.at[t, 1, k], cr.at[t, 1, k], c_id)

        def stage_c(k):
            arrived(gathered.at[t, zpeer[k], across, 1 - core], cs.at[t, 0, k], cr.at[t, 0, k], c_id)
            arrived(
                gathered.at[t, zpeer[k], 1 - across, 1 - core], cs.at[t, 1, k], cr.at[t, 1, k], c_id
            )
            if first and k == 0:
                for d in range(1, devices):
                    source = (me + devices - d) % devices
                    arrived(spread_in.at[source], ss.at[d], sr.at[d], {"expert": source})
                height = own.shape[0]
                turned = jnp.concatenate([spread_in[b] for b in range(devices)], axis=0).T
                for b in range(devices):
                    for at in range(TICKS):
                        scale_ref[at, b * height : (b + 1) * height, :] = turned[
                            at * height : (at + 1) * height, b : b + 1
                        ]
                for load in loads:
                    load.wait()
            group = gathered.at[t, zpeer[k]]
            count = 4 * group.shape[2]
            height = group.shape[2]

            def up_tile(i, carry):
                columns = pl.ds(pl.multiple_of(i * 256, 256), 256)
                inputs = group[...].reshape(count, group.shape[3])
                g = jnp.dot(inputs, gate_w[:, columns], preferred_element_type=jnp.float32)
                u = jnp.dot(inputs, up_w[:, columns], preferred_element_type=jnp.float32)
                hidden[:, columns] = (g / (1.0 + jnp.exp(-g)) * u).astype(jnp.bfloat16)
                return carry

            lax.fori_loop(0, hidden.shape[1] // 256, up_tile, 0)
            start = pl.multiple_of(zpeer[k] * count, count)
            scale = scale_ref[t, pl.ds(start, count), :]

            def down_tile(i, carry):
                columns = pl.ds(pl.multiple_of(i * 256, 256), 256)
                r = jnp.dot(hidden[...], down_w[:, columns], preferred_element_type=jnp.float32)
                r = (r * scale).astype(jnp.bfloat16)
                for xx in range(2):
                    for cc in range(2):
                        at = (xx * 2 + cc) * height
                        part[t, k, cc, xx, :, columns] = r[at : at + height]
                return carry

            lax.fori_loop(0, down_w.shape[1] // 256, down_tile, 0)
            send(part.at[t, k, 1 - core], core_in.at[t, k], ps.at[t, k], pr.at[t, k], c_id)

        def stage_d(k):
            arrived(core_in.at[t, k], ps.at[t, k], pr.at[t, k], c_id)
            chip_sum[t, k] = (
                part[t, k, core].astype(jnp.float32) + core_in[t, k].astype(jnp.float32)
            ).astype(jnp.bfloat16)
            send(chip_sum.at[t, k, 1 - across], x_in.at[t, k], qs.at[t, k], qr.at[t, k], x_id)

        def stage_e(k):
            arrived(x_in.at[t, k], qs.at[t, k], qr.at[t, k], x_id)
            pair_sum[t, k] = (
                chip_sum[t, k, across].astype(jnp.float32) + x_in[t, k].astype(jnp.float32)
            ).astype(jnp.bfloat16)
            if k:
                send(pair_sum.at[t, k], z_in.at[t, lane[k]], ts.at[t, k], tr.at[t, lane[k]], z_ids[k])

        for step in range(NZ + 3):
            for lag, stage in ((0, stage_a), (1, stage_b), (2, stage_d), (3, stage_e), (1, stage_c)):
                if 0 <= step - lag < NZ:
                    stage(step - lag)

        total = as_float + pair_sum[t, 0].astype(jnp.float32)
        for k in range(1, NZ):
            arrived(z_in.at[t, k], ts.at[t, k], tr.at[t, k], z_ids[k])
            total = total + z_in[t, k].astype(jnp.float32)
        out_ref[t] = total.astype(jnp.bfloat16)

    run_tick(0, True)
    carry = pltpu.make_async_remote_copy(
        src_ref=out_ref.at[0], dst_ref=held_next, send_sem=hs, recv_sem=hr,
        device_id=s_id, device_id_type=pl.DeviceIdType.MESH,
    )

    @pl.when(section == 0)
    def _():
        carry.start()
        held_next[...] = entering_ref[...]

    @pl.when(section == 1)
    def _():
        carry.wait_recv()

    run_tick(1, False)

    @pl.when(section == 0)
    def _():
        carry.wait_send()

    for copy in sends:
        copy.wait_send()

    @pl.when(inner == 1)
    def _():
        for args in inner_sends:
            describe(*args).wait_send()


def layers_call(held, entering, gain, spread, gate_w, up_w, down_w):
    rows, width = held.shape
    inner = gate_w.shape[1]
    bf16 = jnp.bfloat16
    dma = pltpu.SemaphoreType.DMA
    vmem = pl.BlockSpec(memory_space=pltpu.VMEM)
    hbm = pl.BlockSpec(memory_space=pl.ANY)
    tall = TICKS * 16 * rows
    return pl.pallas_call(
        layers_kernel,
        out_shape=jax.ShapeDtypeStruct((TICKS, rows, width), bf16),
        in_specs=[vmem] * 4 + [hbm] * 3,
        out_specs=vmem,
        scratch_shapes=[
            pltpu.VMEM((TICKS, NZ, 2, 2, rows, width), bf16),
            pltpu.VMEM((rows, width), bf16),
            pltpu.VMEM((4 * rows, inner), bf16),
            pltpu.VMEM((TICKS, NZ, 2, 2, rows, width), bf16),
            pltpu.VMEM((TICKS, NZ, 2, rows, width), bf16),
            pltpu.VMEM((TICKS, NZ, 2, rows, width), bf16),
            pltpu.VMEM((TICKS, NZ, rows, width), bf16),
            pltpu.VMEM((TICKS, NZ, rows, width), bf16),
            pltpu.VMEM((TICKS, NZ, rows, width), bf16),
            pltpu.VMEM(gate_w.shape, bf16),
            pltpu.VMEM(up_w.shape, bf16),
            pltpu.VMEM(down_w.shape, bf16),
            pltpu.VMEM((4 * NZ, 1, TICKS * rows), jnp.float32),
            pltpu.VMEM((TICKS, 4 * NZ * rows, 1), jnp.float32),
            dma((3,)),
            dma((4 * NZ,)), dma((4 * NZ,)),
            dma((TICKS, NZ + 1)), dma((TICKS, NZ)),
            dma((TICKS, NZ)), dma((TICKS, NZ)),
            dma((TICKS, 2, NZ)), dma((TICKS, 2, NZ)),
            dma((TICKS, NZ)), dma((TICKS, NZ)),
            dma((TICKS, NZ)), dma((TICKS, NZ)),
            dma((TICKS, NZ)), dma((TICKS, NZ)),
            dma, dma,
        ],
        compiler_params=pltpu.CompilerParams(
            collective_id=0, has_side_effects=True, vmem_limit_bytes=58 * 2**20
        ),
        cost_estimate=pl.CostEstimate(
            flops=6 * tall * width * inner,
            bytes_accessed=6 * width * inner + 8 * rows * width,
            transcendentals=tall * inner,
        ),
    )(held, entering, gain, spread, gate_w, up_w, down_w)


def local(in_flight, entering, norm_gain, w_gate, w_up, w_down, routes, combine_weight):
    section_index = lax.axis_index("section")
    experts = lax.axis_size("expert") * w_gate.shape[1]
    spread = expert_weights(routes[0], combine_weight[0], experts)
    if experts == 4 * NZ and lax.axis_size("section") == 2:
        return layers_call(
            in_flight[0], entering[0], norm_gain, spread.reshape(-1, experts).T[:, None],
            w_gate[0, 0], w_up[0, 0], w_down[0, 0],
        )[:, None]
    mine = lax.all_to_all(spread, "expert", split_axis=2, concat_axis=1, tiled=True)
    carried = in_flight[0]
    traced = []
    for tick_index in range(TICKS):
        layer_out = gathered_layer(
            carried, norm_gain[0], mine[tick_index], w_gate[0, 0], w_up[0, 0], w_down[0, 0]
        )
        traced.append(layer_out)
        if tick_index + 1 < TICKS:
            shifted = passed_along(layer_out, "section", 1)
            carried = jnp.where(section_index == 0, entering[tick_index], shifted)
    return jnp.stack(traced)[:, None]


def solution(mesh):
    placed = (
        P("section", "expert", None),
        P(None, "expert", None),
        P("section", None),
        P("section", "expert", None, None),
        P("section", "expert", None, None),
        P("section", "expert", None, None),
        P("section", None, "expert", None),
        P("section", None, "expert", None),
    )
    return jax.shard_map(
        local,
        mesh=mesh,
        in_specs=placed,
        out_specs=P(None, "section", "expert", None),
        check_vma=False,
    )
```

```python
import jax
import jax.numpy as jnp
from jax import lax
from jax.experimental import pallas as pl
from jax.experimental.pallas import tpu as pltpu
from jax.sharding import PartitionSpec as P

TICKS = 2
EPSILON = 1e-06


def passed_along(x, axis, by):
    devices = lax.axis_size(axis)
    pairs = [(i, i + by) for i in range(devices) if 0 <= i + by < devices]
    return lax.ppermute(x, axis, pairs)


def rms_normed(hidden_rows, norm_gain):
    as_float = hidden_rows.astype(jnp.float32)
    inv_scale = lax.rsqrt(jnp.mean(as_float * as_float, axis=-1, keepdims=True) + EPSILON)
    return (as_float * inv_scale * norm_gain.astype(jnp.float32)).astype(jnp.bfloat16)


def expert_weights(routes, combine, experts):
    hits = routes[..., None] == jnp.arange(experts, dtype=jnp.int32)
    return jnp.sum(jnp.where(hits, combine[..., None], 0.0), axis=-2)


def gathered_layer(hidden_rows, norm_gain, scales, gate_w, up_w, down_w):
    normed = rms_normed(hidden_rows, norm_gain)
    inputs = lax.all_gather(normed, "expert", axis=0, tiled=True)
    gate_sum = jnp.dot(inputs, gate_w, preferred_element_type=jnp.float32)
    up_sum = jnp.dot(inputs, up_w, preferred_element_type=jnp.float32)
    hidden = (jax.nn.silu(gate_sum) * up_sum).astype(jnp.bfloat16)
    result = jnp.dot(hidden, down_w, preferred_element_type=jnp.float32)
    scaled = (result * scales).astype(jnp.bfloat16)
    summed = lax.psum_scatter(scaled, "expert", scatter_dimension=0, tiled=True)
    return (hidden_rows.astype(jnp.float32) + summed.astype(jnp.float32)).astype(jnp.bfloat16)


NZ = 4


def layers_kernel(
    x_ref, entering_ref, gain_ref, spread_ref, gate_hbm, up_hbm, down_hbm, out_ref,
    gathered, held_next, hidden, part, core_in, chip_sum, x_in, pair_sum, z_in,
    gate_w, up_w, down_w, spread_in, scale_ref,
    w_sem, ss, sr, zs, zr, xs, xr, cs, cr, ps, pr, qs, qr, ts, tr, hs, hr,
):
    section = lax.axis_index("section")
    me = lax.axis_index("expert")
    core = me % 2
    across = (me // 2) % 2
    z = me // 4
    inner = ((z + 1) // 2) % 2
    near, skip, mirror = z + 1 - 2 * (z % 2), (z + 2) % 4, 3 - z
    zpeer = [
        z,
        near,
        (1 - inner) * skip + inner * mirror,
        (1 - inner) * mirror + inner * skip,
    ]
    lane = [0, 1, 2 + inner, 3 - inner]
    devices = 4 * NZ

    def expert_id(zz, xx, cc):
        return {"expert": zz * 4 + xx * 2 + cc}

    z_ids = [expert_id(zpeer[d], across, core) for d in range(NZ)]
    x_id = expert_id(z, 1 - across, core)
    c_id = expert_id(z, across, 1 - core)
    s_id = {"section": 1 - section}

    loads = [
        pltpu.make_async_copy(src, dst, w_sem.at[i])
        for i, (src, dst) in enumerate(((gate_hbm, gate_w), (up_hbm, up_w), (down_hbm, down_w)))
    ]
    for load in loads:
        load.start()

    barrier = pltpu.get_barrier_semaphore()
    others = [{"expert": (me + d) % devices} for d in range(1, devices)]
    for peer in others + [s_id]:
        pl.semaphore_signal(barrier, inc=1, device_id=peer, device_id_type=pl.DeviceIdType.MESH)
    spread_in[me] = spread_ref[me]

    sends = []
    inner_sends = []

    def describe(src, dst, s_sem, r_sem, peer):
        return pltpu.make_async_remote_copy(
            src_ref=src, dst_ref=dst, send_sem=s_sem, recv_sem=r_sem,
            device_id=peer, device_id_type=pl.DeviceIdType.MESH,
        )

    def begin(*args):
        copy = describe(*args)
        copy.start()
        return copy

    def send(*args):
        sends.append(begin(*args))

    def send_inner(*args):
        @pl.when(inner == 1)
        def _():
            begin(*args)

        inner_sends.append(args)

    def arrived(ref, s_sem, r_sem, peer):
        pltpu.make_async_remote_copy(
            src_ref=ref, dst_ref=ref, send_sem=s_sem, recv_sem=r_sem,
            device_id=peer, device_id_type=pl.DeviceIdType.MESH,
        ).wait_recv()

    def run_tick(t, first):
        rows = x_ref[...] if t == 0 else held_next[...]
        as_float = rows.astype(jnp.float32)
        inv = lax.rsqrt(jnp.mean(as_float * as_float, axis=-1, keepdims=True) + EPSILON)
        own = gathered.at[t, z, across, core]
        own[...] = (as_float * inv * gain_ref[...].astype(jnp.float32)).astype(jnp.bfloat16)
        if first:
            pl.semaphore_wait(barrier, devices)
        send(own, own, zs.at[t, 0], zr.at[t, 1], z_ids[1])
        send_inner(own, own, zs.at[t, 1], zr.at[t, 2], z_ids[2])

        def stage_a(k):
            mine = gathered.at[t, zpeer[k], across, core]
            if k:
                arrived(mine, zs.at[t, 0], zr.at[t, k], z_ids[k])
                if k == 1:
                    send_inner(mine, mine, zs.at[t, 2], zr.at[t, 3], z_ids[2])
                else:
                    send_inner(mine, mine, zs.at[t, k + 1], zr.at[t, k], z_ids[1])
            send(mine, mine, xs.at[t, k], xr.at[t, k], x_id)
            send(mine, mine, cs.at[t, 0, k], cr.at[t, 0, k], c_id)

            if first and k == 0:
                for d in range(1, devices):
                    peer = (me + d) % devices
                    send(spread_ref.at[peer], spread_in.at[me], ss.at[d], sr.at[d], {"expert": peer})

        def stage_b(k):
            other = gathered.at[t, zpeer[k], 1 - across, core]
            arrived(other, xs.at[t, k], xr.at[t, k], x_id)
            send(other, other, cs.at[t, 1, k], cr.at[t, 1, k], c_id)

        def stage_c(k):
            arrived(gathered.at[t, zpeer[k], across, 1 - core], cs.at[t, 0, k], cr.at[t, 0, k], c_id)
            arrived(
                gathered.at[t, zpeer[k], 1 - across, 1 - core], cs.at[t, 1, k], cr.at[t, 1, k], c_id
            )
            if first and k == 1:
                for d in range(1, devices):
                    source = (me + devices - d) % devices
                    arrived(spread_in.at[source], ss.at[d], sr.at[d], {"expert": source})
                height = own.shape[0]
                turned = jnp.concatenate([spread_in[b] for b in range(devices)], axis=0).T
                for b in range(devices):
                    for at in range(TICKS):
                        scale_ref[at, b * height : (b + 1) * height, :] = turned[
                            at * height : (at + 1) * height, b : b + 1
                        ]
                for load in loads:
                    load.wait()
            group = gathered.at[t, zpeer[k]]
            count = 4 * group.shape[2]
            height = group.shape[2]

            def up_tile(i, carry):
                columns = pl.ds(pl.multiple_of(i * 256, 256), 256)
                inputs = group[...].reshape(count, group.shape[3])
                g = jnp.dot(inputs, gate_w[:, columns], preferred_element_type=jnp.float32)
                u = jnp.dot(inputs, up_w[:, columns], preferred_element_type=jnp.float32)
                hidden[:, columns] = (g / (1.0 + jnp.exp(-g)) * u).astype(jnp.bfloat16)
                return carry

            lax.fori_loop(0, hidden.shape[1] // 256, up_tile, 0)
            start = pl.multiple_of(zpeer[k] * count, count)
            scale = scale_ref[t, pl.ds(start, count), :]

            def down_tile(i, carry):
                columns = pl.ds(pl.multiple_of(i * 256, 256), 256)
                r = jnp.dot(hidden[...], down_w[:, columns], preferred_element_type=jnp.float32)
                r = (r * scale).astype(jnp.bfloat16)
                for xx in range(2):
                    for cc in range(2):
                        at = (xx * 2 + cc) * height
                        part[t, k, cc, xx, :, columns] = r[at : at + height]
                return carry

            lax.fori_loop(0, down_w.shape[1] // 256, down_tile, 0)
            send(part.at[t, k, 1 - core], core_in.at[t, k], ps.at[t, k], pr.at[t, k], c_id)

        def stage_d(k):
            arrived(core_in.at[t, k], ps.at[t, k], pr.at[t, k], c_id)
            chip_sum[t, k] = (
                part[t, k, core].astype(jnp.float32) + core_in[t, k].astype(jnp.float32)
            ).astype(jnp.bfloat16)
            send(chip_sum.at[t, k, 1 - across], x_in.at[t, k], qs.at[t, k], qr.at[t, k], x_id)

        def stage_e(k):
            arrived(x_in.at[t, k], qs.at[t, k], qr.at[t, k], x_id)
            pair_sum[t, k] = (
                chip_sum[t, k, across].astype(jnp.float32) + x_in[t, k].astype(jnp.float32)
            ).astype(jnp.bfloat16)
            if k:
                send(pair_sum.at[t, k], z_in.at[t, lane[k]], ts.at[t, k], tr.at[t, lane[k]], z_ids[k])

        for step in range(NZ + 4):
            for lag, stage in ((0, stage_a), (1, stage_b), (3, stage_d), (4, stage_e), (2, stage_c)):
                if 0 <= step - lag < NZ:
                    stage(step - lag if lag < 2 else (step - lag + 1) % NZ)

        total = as_float + pair_sum[t, 0].astype(jnp.float32)
        for k in range(1, NZ):
            arrived(z_in.at[t, k], ts.at[t, k], tr.at[t, k], z_ids[k])
            total = total + z_in[t, k].astype(jnp.float32)
        out_ref[t] = total.astype(jnp.bfloat16)

    run_tick(0, True)
    carry = pltpu.make_async_remote_copy(
        src_ref=out_ref.at[0], dst_ref=held_next, send_sem=hs, recv_sem=hr,
        device_id=s_id, device_id_type=pl.DeviceIdType.MESH,
    )

    @pl.when(section == 0)
    def _():
        carry.start()
        held_next[...] = entering_ref[...]

    @pl.when(section == 1)
    def _():
        carry.wait_recv()

    run_tick(1, False)

    @pl.when(section == 0)
    def _():
        carry.wait_send()

    for copy in sends:
        copy.wait_send()

    @pl.when(inner == 1)
    def _():
        for args in inner_sends:
            describe(*args).wait_send()


def layers_call(held, entering, gain, spread, gate_w, up_w, down_w):
    rows, width = held.shape
    inner = gate_w.shape[1]
    bf16 = jnp.bfloat16
    dma = pltpu.SemaphoreType.DMA
    vmem = pl.BlockSpec(memory_space=pltpu.VMEM)
    hbm = pl.BlockSpec(memory_space=pl.ANY)
    tall = TICKS * 16 * rows
    return pl.pallas_call(
        layers_kernel,
        out_shape=jax.ShapeDtypeStruct((TICKS, rows, width), bf16),
        in_specs=[vmem] * 4 + [hbm] * 3,
        out_specs=vmem,
        scratch_shapes=[
            pltpu.VMEM((TICKS, NZ, 2, 2, rows, width), bf16),
            pltpu.VMEM((rows, width), bf16),
            pltpu.VMEM((4 * rows, inner), bf16),
            pltpu.VMEM((TICKS, NZ, 2, 2, rows, width), bf16),
            pltpu.VMEM((TICKS, NZ, 2, rows, width), bf16),
            pltpu.VMEM((TICKS, NZ, 2, rows, width), bf16),
            pltpu.VMEM((TICKS, NZ, rows, width), bf16),
            pltpu.VMEM((TICKS, NZ, rows, width), bf16),
            pltpu.VMEM((TICKS, NZ, rows, width), bf16),
            pltpu.VMEM(gate_w.shape, bf16),
            pltpu.VMEM(up_w.shape, bf16),
            pltpu.VMEM(down_w.shape, bf16),
            pltpu.VMEM((4 * NZ, 1, TICKS * rows), jnp.float32),
            pltpu.VMEM((TICKS, 4 * NZ * rows, 1), jnp.float32),
            dma((3,)),
            dma((4 * NZ,)), dma((4 * NZ,)),
            dma((TICKS, NZ + 1)), dma((TICKS, NZ)),
            dma((TICKS, NZ)), dma((TICKS, NZ)),
            dma((TICKS, 2, NZ)), dma((TICKS, 2, NZ)),
            dma((TICKS, NZ)), dma((TICKS, NZ)),
            dma((TICKS, NZ)), dma((TICKS, NZ)),
            dma((TICKS, NZ)), dma((TICKS, NZ)),
            dma, dma,
        ],
        compiler_params=pltpu.CompilerParams(
            collective_id=0, has_side_effects=True, vmem_limit_bytes=58 * 2**20
        ),
        cost_estimate=pl.CostEstimate(
            flops=6 * tall * width * inner,
            bytes_accessed=6 * width * inner + 8 * rows * width,
            transcendentals=tall * inner,
        ),
    )(held, entering, gain, spread, gate_w, up_w, down_w)


def local(in_flight, entering, norm_gain, w_gate, w_up, w_down, routes, combine_weight):
    section_index = lax.axis_index("section")
    experts = lax.axis_size("expert") * w_gate.shape[1]
    spread = expert_weights(routes[0], combine_weight[0], experts)
    if experts == 4 * NZ and lax.axis_size("section") == 2:
        return layers_call(
            in_flight[0], entering[0], norm_gain, spread.reshape(-1, experts).T[:, None],
            w_gate[0, 0], w_up[0, 0], w_down[0, 0],
        )[:, None]
    mine = lax.all_to_all(spread, "expert", split_axis=2, concat_axis=1, tiled=True)
    carried = in_flight[0]
    traced = []
    for tick_index in range(TICKS):
        layer_out = gathered_layer(
            carried, norm_gain[0], mine[tick_index], w_gate[0, 0], w_up[0, 0], w_down[0, 0]
        )
        traced.append(layer_out)
        if tick_index + 1 < TICKS:
            shifted = passed_along(layer_out, "section", 1)
            carried = jnp.where(section_index == 0, entering[tick_index], shifted)
    return jnp.stack(traced)[:, None]


def solution(mesh):
    placed = (
        P("section", "expert", None),
        P(None, "expert", None),
        P("section", None),
        P("section", "expert", None, None),
        P("section", "expert", None, None),
        P("section", "expert", None, None),
        P("section", None, "expert", None),
        P("section", None, "expert", None),
    )
    return jax.shard_map(
        local,
        mesh=mesh,
        in_specs=placed,
        out_specs=P(None, "section", "expert", None),
        check_vma=False,
    )
```
